512 devices in a mesh: prow: 32 (over x_lo, z, core), pcol: 16 (over y, x_hi).
Axes of the slice: x: 4 (x_hi: 2, x_lo: 2; x = x_hi * 2 + x_lo), y: 8, z: 8, core: 2. Of those that a mesh axis runs over, the one named last changes fastest.
Arguments:
- reduced_vectors: float32 [98304, 2048], P('prow', 'pcol'), may hold values from -6 to 6
- panel_one: float32 [98304, 256], P(('prow', 'pcol')), may hold values from -0.01953125 to 0.01953125
- factor_one: float32 [256, 256], P('pcol'), as said below
- panel_two: float32 [98304, 256], P(('prow', 'pcol')), may hold values from -0.01953125 to 0.01953125
- factor_two: float32 [256, 256], P('pcol'), as said below
Outputs:
- eigenvectors: float32 [98304, 2048], P('prow', 'pcol')
The draws below stay inside these ranges and needn't reach their ends.
Inputs may be any that keep to these rules, and one draw needn't show every extreme that they name: factor_one is upper triangular with its diagonal between 1 and 2. factor_two is upper triangular with its diagonal between 1 and 2.
All inputs are finite; a program needn't handle non-finite values.
Results may differ from the reference program's by a relative error of at most 0.00007.
Values sent between devices are 32-bit elements; how exact they have to be, the bound alone decides.
No kernel may reach another device: no remote copies, remote signals or barrier semaphores. Data moves between devices by JAX's collectives and lax.ppermute only.
A program may use at most 64 MiB of HBM per device.

```python
import jax
import jax.numpy as jnp
from jax import lax

N = 98304
NB = 256
K = 2048


def upper_factor(key):
    diag_key, off_key = jax.random.split(key)
    diagonal = jax.random.uniform(diag_key, (NB,), jnp.float32, 1.0, 2.0)
    off_part = 0.1 * jax.random.normal(off_key, (NB, NB), jnp.float32)
    row_index = jnp.arange(NB)[:, None]
    col_index = jnp.arange(NB)[None, :]
    strict = jnp.where(col_index > row_index, off_part, 0.0)
    return strict + jnp.diag(diagonal)


def draw_factor_one(key, part):
    key = jax.random.fold_in(key, 11)
    return upper_factor(key)


def draw_factor_two(key, part):
    key = jax.random.fold_in(key, 23)
    return upper_factor(key)


def block_scale(own_key, shape, cuts, smallest, largest):
    gain, own = 1.0, jax.random.fold_in(own_key, 6)
    for position, shards_of in cuts:
        steps = jnp.exp(jax.random.uniform(jax.random.fold_in(own, position), (shards_of,), jnp.float32, smallest / len(cuts), largest / len(cuts)))
        gain = gain * jnp.repeat(steps, shape[position] // shards_of).reshape([-1 if axis == position else 1 for axis in range(len(shape))])
    return gain


def centred(rng, dims, scale, bound, pieces=(), kind=jnp.bfloat16):
    drawn = jax.random.normal(rng, dims, jnp.float32) * scale
    if len(pieces) > 0:
        drawn = block_scale(rng, dims, pieces, -0.22, 0.18) * drawn
    return jnp.clip(drawn, min=-bound, max=bound).astype(kind)


def setup_inputs(seed: int = 0) -> dict:
    keys = jax.random.split(jax.random.key(seed), 6)
    reduced_vectors = centred(keys[0], (N, K), 1.0, 6.0, ((0, 32), (1, 16)), jnp.float32)
    panel_one = centred(keys[1], (N, NB), N ** -0.5, 0.01953125, ((0, 512),), jnp.float32)
    factor_one = draw_factor_one(jax.random.fold_in(keys[5], 71), 0)
    panel_two = centred(keys[3], (N, NB), N ** -0.5, 0.01953125, ((0, 512),), jnp.float32)
    factor_two = draw_factor_two(jax.random.fold_in(keys[5], 71), 0)
    return dict(reduced_vectors=reduced_vectors, panel_one=panel_one, factor_one=factor_one, panel_two=panel_two, factor_two=factor_two)


def matmul_hi(left, right):
    return jnp.dot(left, right, precision=lax.Precision.HIGHEST, preferred_element_type=jnp.float32)


def reflect(current, panel, factor):
    inner_prod = matmul_hi(panel.T, current)
    coeffs = matmul_hi(factor, inner_prod)
    return current - matmul_hi(panel, coeffs)


def reference(reduced_vectors, panel_one, factor_one, panel_two, factor_two):
    middle = reflect(reduced_vectors, panel_two, factor_two)
    return reflect(middle, panel_one, factor_one)
```

```python
import jax
import jax.numpy as jnp
from jax import lax
from jax.sharding import Mesh
from jax.sharding import PartitionSpec as P

AXES = ("xl", "z", "core", "y", "xh")
SIZES = (2, 8, 2, 8, 2)
NY = 8


def dot(left, right, dims):
    return lax.dot_general(
        left,
        right,
        (dims, ((), ())),
        precision=lax.Precision.HIGH,
        preferred_element_type=jnp.float32,
    )


def swap(value, axis):
    return lax.ppermute(value, axis, [(0, 1), (1, 0)])


def step_up(value):
    return lax.ppermute(value, "y", [(i, (i + 1) % NY) for i in range(NY)])


def step_down(value):
    return lax.ppermute(value, "y", [(i, (i - 1) % NY) for i in range(NY)])


def pair_up(own):
    other = swap(own, "xh")
    first = lax.axis_index("xh") == 0
    return jnp.stack([jnp.where(first, own, other), jnp.where(first, other, own)])


def ring(own):
    blocks = [None] * NY
    blocks[0] = own
    up = down = own
    for step in range(1, 4):
        up, down = step_up(up), step_down(down)
        blocks[NY - step], blocks[step] = up, down
    low, high = step_up(up[0]), step_down(down[1])
    blocks[4] = jnp.stack([low, high])
    return blocks


def all_sum(partial_value):
    rows = partial_value.shape[0] // 16
    parts = lax.all_to_all(
        partial_value.reshape(16, rows, 128), ("z", "core"), 0, 0
    ).sum(0)
    parts = parts + swap(parts, "xl")
    spread = jnp.broadcast_to(parts[None], (16, rows, 128))
    return lax.all_to_all(spread, ("z", "core"), 0, 0).reshape(16 * rows, 128)


def shards(vectors, panel_one, factor_one, panel_two, factor_two):
    here = lax.axis_index("y")
    rows = panel_one.shape[0]
    two = ring(pair_up(jnp.concatenate([panel_two, factor_two])))
    one = ring(pair_up(jnp.concatenate([panel_one, factor_one])))

    by_owner = vectors.reshape(NY, 2, rows, 128)
    rolled = lax.dynamic_slice_in_dim(
        jnp.concatenate([by_owner, by_owner]), here, NY, 0
    )
    both = ((0, 1), (0, 1))
    inner_two = inner_one = cross = 0.0
    for k in range(NY):
        part_two, part_one = two[k][:, :rows], one[k][:, :rows]
        inner_two = inner_two + dot(part_two, rolled[k], both)
        inner_one = inner_one + dot(part_one, rolled[k], both)
        cross = cross + dot(part_one, part_two, both)
    sums = all_sum(
        jnp.concatenate([inner_two, inner_one, cross[:, :128], cross[:, 128:]])
    )
    inner_two, inner_one = sums[:256], sums[256:512]
    cross = jnp.concatenate([sums[512:768], sums[768:]], axis=1)

    def whole(blocks):
        tri = jnp.concatenate([b[:, rows:].reshape(-1, 256) for b in blocks])
        tri = jnp.concatenate([tri, tri])
        return lax.dynamic_slice_in_dim(tri, (NY - here) % NY * 32, 256, 0)

    plain = ((1,), (0,))
    coeff_two = dot(whole(two), inner_two, plain)
    coeff_one = dot(whole(one), inner_one - dot(cross, coeff_two, plain), plain)
    out = [
        rolled[k]
        - dot(two[k][:, :rows], coeff_two, ((2,), (0,)))
        - dot(one[k][:, :rows], coeff_one, ((2,), (0,)))
        for k in range(NY)
    ]
    out = jnp.stack(out + out)
    out = lax.dynamic_slice_in_dim(out, (NY - here) % NY, NY, 0)
    return out.reshape(vectors.shape)


def solution(mesh):
    fine = Mesh(mesh.devices.reshape(SIZES), AXES)
    prow, pcol = ("xl", "z", "core"), ("y", "xh")
    in_specs = (
        P(prow, pcol),
        P(prow + pcol, None),
        P(pcol, None),
        P(prow + pcol, None),
        P(pcol, None),
    )
    return jax.shard_map(
        shards,
        mesh=fine,
        in_specs=in_specs,
        out_specs=P(prow, pcol),
        check_vma=False,
    )
```

```python
import functools

import jax
import jax.numpy as jnp
from jax import lax
from jax.experimental import pallas as pl
from jax.experimental.pallas import tpu as pltpu
from jax.sharding import Mesh
from jax.sharding import PartitionSpec as P

AXES = ("xl", "z", "core", "y", "xh")
SIZES = (2, 8, 2, 8, 2)
NY = 8
ROWS = 192
PLAIN = ((1,), (0,))
LIMIT = 60 * 1024 * 1024


def dot(left, right, dims):
    return lax.dot_general(
        left,
        right,
        (dims, ((), ())),
        precision=lax.Precision.HIGH,
        preferred_element_type=jnp.float32,
    )


def swap(value, axis):
    return lax.ppermute(value, axis, [(0, 1), (1, 0)])


def after(value, *earlier):
    return lax.optimization_barrier((value, *earlier))[0]


def split(value):
    high = value.astype(jnp.bfloat16)
    return high, (value - high.astype(jnp.float32)).astype(jnp.bfloat16)


def pack_kernel(core_ref, one_ref, two_ref, tri_one_ref, tri_two_ref, out_ref):
    out_ref[:ROWS, :256] = one_ref[...]
    out_ref[:ROWS, 256:] = two_ref[...]
    tri = jnp.where(core_ref[0] == 0, tri_one_ref[...], tri_two_ref[...])
    out_ref[ROWS:, :256] = tri[:8]
    out_ref[ROWS:, 256:] = tri[8:]


def pack(core, panel_one, panel_two, factor_one, factor_two):
    vmem = pl.BlockSpec(memory_space=pltpu.VMEM)
    return pl.pallas_call(
        pack_kernel,
        out_shape=jax.ShapeDtypeStruct((ROWS + 8, 512), jnp.float32),
        in_specs=[pl.BlockSpec(memory_space=pltpu.SMEM)] + [vmem] * 4,
        out_specs=vmem,
        name="pack",
    )(core, panel_one, panel_two, factor_one, factor_two)


def products_kernel(
    place_ref, near_ref, mine_ref, seen_ref, keep_ref, send_ref, inner, cross
):
    side, core = place_ref[0], place_ref[1]
    step = pl.program_id(0)
    count = near_ref.shape[0]
    left = near_ref[:, :ROWS, :].reshape(count * ROWS, 512)
    right = jnp.concatenate(
        [
            mine_ref[:, side].reshape(count * ROWS, 128),
            seen_ref[...].reshape(count * ROWS, 128),
        ],
        axis=1,
    )
    high, low = split(left)
    right_high, right_low = split(right)
    by_rows = (((0,), (0,)), ((), ()))

    def triple(a, a_low, b, b_low):
        return lax.dot_general(
            jnp.concatenate([a, a, a_low]),
            jnp.concatenate([b, b_low, b]),
            by_rows,
            preferred_element_type=jnp.float32,
        )

    inner_part = triple(high, low, right_high, right_low)
    cross_part = triple(high[:, :256], low[:, :256], high[:, 256:], low[:, 256:])
    inner_part = inner_part.reshape(2, 256, 256)
    cross_part = cross_part.reshape(2, 128, 256)

    @pl.when(step == 0)
    def _():
        inner[...] = inner_part
        cross[...] = cross_part

    @pl.when(step > 0)
    def _():
        inner[...] += inner_part
        cross[...] += cross_part

    @pl.when(step == pl.num_programs(0) - 1)
    def _():
        for out_ref, which in ((keep_ref, core), (send_ref, 1 - core)):
            out_ref[:256] = inner[which, :, :128]
            out_ref[256:512] = inner[which, :, 128:]
            out_ref[512:640] = cross[which, :, :128]
            out_ref[640:] = cross[which, :, 128:]


def products(place, near, by_owner, seen):
    count = 4
    return pl.pallas_call(
        products_kernel,
        grid=(NY // count,),
        out_shape=[jax.ShapeDtypeStruct((768, 128), jnp.float32)] * 2,
        in_specs=[
            pl.BlockSpec(memory_space=pltpu.SMEM),
            pl.BlockSpec((count, ROWS + 8, 512), lambda i: (i, 0, 0)),
            pl.BlockSpec((count, 2, ROWS, 128), lambda i: (i, 0, 0, 0)),
            pl.BlockSpec((count, ROWS, 128), lambda i: (i, 0, 0)),
        ],
        out_specs=[pl.BlockSpec((768, 128), lambda i: (0, 0))] * 2,
        scratch_shapes=[
            pltpu.VMEM((2, 256, 256), jnp.float32),
            pltpu.VMEM((2, 128, 256), jnp.float32),
        ],
        compiler_params=pltpu.CompilerParams(vmem_limit_bytes=LIMIT),
        name="products",
    )(place, near, by_owner, seen)


def update_kernel(place_ref, near_ref, far_ref, coeff_ref, old_ref, out_ref):
    side = place_ref[0]
    count = near_ref.shape[0]
    high, low = split(coeff_ref[...])
    both = jnp.concatenate([high, low], axis=1)
    for ref, which in ((near_ref, side), (far_ref, 1 - side)):
        panel = ref[:, :ROWS, :].reshape(count * ROWS, 512)
        panel_high, panel_low = split(panel)
        main = jnp.dot(panel_high, both, preferred_element_type=jnp.float32)
        rest = jnp.dot(panel_low, high, preferred_element_type=jnp.float32)
        change = main[:, :128] + (main[:, 128:] + rest)
        out_ref[:, which] = old_ref[:, which] - change.reshape(count, ROWS, 128)


def update(place, near, far, coeffs, by_owner):
    count = 2
    return pl.pallas_call(
        update_kernel,
        grid=(NY // count,),
        out_shape=jax.ShapeDtypeStruct(by_owner.shape, jnp.float32),
        in_specs=[
            pl.BlockSpec(memory_space=pltpu.SMEM),
            pl.BlockSpec((count, ROWS + 8, 512), lambda i: (i, 0, 0)),
            pl.BlockSpec((count, ROWS, 512), lambda i: (i, 0, 0)),
            pl.BlockSpec((512, 128), lambda i: (0, 0)),
            pl.BlockSpec((count, 2, ROWS, 128), lambda i: (i, 0, 0, 0)),
        ],
        out_specs=pl.BlockSpec((count, 2, ROWS, 128), lambda i: (i, 0, 0, 0)),
        compiler_params=pltpu.CompilerParams(vmem_limit_bytes=LIMIT),
        name="update",
    )(place, near, far, coeffs, by_owner)


def shards(vectors, panel_one, factor_one, panel_two, factor_two):
    side, core = lax.axis_index("xh"), lax.axis_index("core")
    place = jnp.stack([side, core]).astype(jnp.int32)

    own = pack(core[None], panel_one, panel_two, factor_one, factor_two)
    near = lax.all_gather(own, "y", axis=0)
    by_owner = vectors.reshape(NY, 2, ROWS, 128)
    theirs = lax.dynamic_index_in_dim(by_owner, 1 - side, 1, False)
    seen = swap(theirs, "xh")
    far = lax.all_gather(swap(own[:ROWS], "xh"), "y", axis=0)

    keep, send = products(place, near, by_owner, seen)
    part = keep + swap(send, "core")
    other = swap(part[256:], "xh")
    part = jnp.concatenate([part[:256] + other[:256], part[512:] + other[256:]])
    piece = lax.all_to_all(part.reshape(16, 32, 128), ("xl", "z"), 0, 0).sum(0)
    spread = jnp.broadcast_to(piece[None], (16, 32, 128))
    part = lax.all_to_all(spread, ("xl", "z"), 0, 0).reshape(512, 128)

    tri = near[:, ROWS:]
    tri = jnp.concatenate([tri[..., :256], tri[..., 256:]], axis=1)
    tri = lax.all_gather(tri, "core", axis=0)
    other = swap(tri, "xh")
    tri = jnp.where(
        side == 0,
        jnp.stack([tri, other], axis=2),
        jnp.stack([other, tri], axis=2),
    ).reshape(2, 256, 256)

    both = lax.all_gather(part, "core", axis=0)
    cross = jnp.concatenate([both[:, 256:384], both[:, 384:]], axis=2)
    inner_one, inner_two, cross = both[0, :256], both[1, :256], cross.reshape(256, 256)
    coeff_two = dot(tri[1], inner_two, PLAIN)
    coeff_one = dot(tri[0], inner_one - dot(cross, coeff_two, PLAIN), PLAIN)
    coeffs = jnp.concatenate([coeff_one, coeff_two])
    return update(place, near, far, coeffs, by_owner).reshape(vectors.shape)


def solution(mesh):
    fine = Mesh(mesh.devices.reshape(SIZES), AXES)
    prow, pcol = ("xl", "z", "core"), ("y", "xh")
    in_specs = (
        P(prow, pcol),
        P(prow + pcol, None),
        P(pcol, None),
        P(prow + pcol, None),
        P(pcol, None),
    )
    return jax.shard_map(
        shards,
        mesh=fine,
        in_specs=in_specs,
        out_specs=P(prow, pcol),
        check_vma=False,
    )
```

```python
import functools

import jax
import jax.numpy as jnp
from jax import lax
from jax.experimental import pallas as pl
from jax.experimental.pallas import tpu as pltpu
from jax.sharding import Mesh
from jax.sharding import PartitionSpec as P

AXES = ("xl", "z", "core", "y", "xh")
SIZES = (2, 8, 2, 8, 2)
NY = 8
ROWS = 192
MIB = 1024 * 1024


def swap(value, axis):
    return lax.ppermute(value, axis, [(0, 1), (1, 0)])


def split(value):
    high = value.astype(jnp.bfloat16)
    return high, (value - high.astype(jnp.float32)).astype(jnp.bfloat16)


def pack_kernel(one_ref, two_ref, tri_one_ref, tri_two_ref, out_ref):
    out_ref[:ROWS, :256] = one_ref[...]
    out_ref[:ROWS, 256:] = two_ref[...]
    for i, ref in enumerate((tri_one_ref, tri_two_ref)):
        at = pl.ds(ROWS + 8 * i, 8)
        out_ref[at, :256] = ref[:8]
        out_ref[at, 256:] = ref[8:]


def pack(panel_one, panel_two, factor_one, factor_two):
    vmem = pl.BlockSpec(memory_space=pltpu.VMEM)
    return pl.pallas_call(
        pack_kernel,
        out_shape=jax.ShapeDtypeStruct((ROWS + 16, 512), jnp.float32),
        in_specs=[vmem] * 4,
        out_specs=vmem,
        name="pack",
    )(panel_one, panel_two, factor_one, factor_two)


def products_kernel(
    place_ref, near_ref, mine_ref, seen_ref, keep_ref, send_ref, inner, cross
):
    side, core = place_ref[0], place_ref[1]
    step = pl.program_id(0)
    count = near_ref.shape[0]
    left = near_ref[:, :ROWS, :].reshape(count * ROWS, 512)
    right = jnp.concatenate(
        [
            mine_ref[:, side].reshape(count * ROWS, 128),
            seen_ref[...].reshape(count * ROWS, 128),
        ],
        axis=1,
    )
    high, low = split(left)
    right_high, right_low = split(right)
    by_rows = (((0,), (0,)), ((), ()))

    def triple(a, a_low, b, b_low):
        return lax.dot_general(
            jnp.concatenate([a, a, a_low]),
            jnp.concatenate([b, b_low, b]),
            by_rows,
            preferred_element_type=jnp.float32,
        )

    inner_part = triple(high, low, right_high, right_low)
    cross_part = triple(high[:, :256], low[:, :256], high[:, 256:], low[:, 256:])
    inner_part = inner_part.reshape(2, 256, 256)
    cross_part = cross_part.reshape(2, 128, 256)

    @pl.when(step == 0)
    def _():
        inner[...] = inner_part
        cross[...] = cross_part

    @pl.when(step > 0)
    def _():
        inner[...] += inner_part
        cross[...] += cross_part

    @pl.when(step == pl.num_programs(0) - 1)
    def _():
        for out_ref, which in ((keep_ref, core), (send_ref, 1 - core)):
            own, far = inner[which, :, :128], inner[which, :, 128:]
            out_ref[:256] = jnp.where(side == 0, own, far)
            out_ref[256:512] = jnp.where(side == 0, far, own)
            out_ref[512:640] = cross[which, :, :128]
            out_ref[640:] = cross[which, :, 128:]


def products(place, near, by_owner, seen):
    count = 4
    return pl.pallas_call(
        products_kernel,
        grid=(NY // count,),
        out_shape=[jax.ShapeDtypeStruct((768, 128), jnp.float32)] * 2,
        in_specs=[
            pl.BlockSpec(memory_space=pltpu.SMEM),
            pl.BlockSpec((count, ROWS + 16, 512), lambda i: (i, 0, 0)),
            pl.BlockSpec((count, 2, ROWS, 128), lambda i: (i, 0, 0, 0)),
            pl.BlockSpec((count, ROWS, 128), lambda i: (i, 0, 0)),
        ],
        out_specs=[pl.BlockSpec((768, 128), lambda i: (0, 0))] * 2,
        scratch_shapes=[
            pltpu.VMEM((2, 256, 256), jnp.float32),
            pltpu.VMEM((2, 128, 256), jnp.float32),
        ],
        compiler_params=pltpu.CompilerParams(vmem_limit_bytes=48 * MIB),
        name="products",
    )(place, near, by_owner, seen)


def triple(left, right):
    (high, low), (right_high, right_low) = left, right
    both = jnp.concatenate([right_high, right_low], axis=1)
    main = jnp.dot(high, both, preferred_element_type=jnp.float32)
    rest = jnp.dot(low, right_high, preferred_element_type=jnp.float32)
    return main[:, :128] + (main[:, 128:] + rest)


def update_kernel(
    place_ref, near_ref, far_ref, sums_ref, near_tri_ref, far_tri_ref, old_ref,
    out_ref, coeffs, tri,
):
    side = place_ref[0]
    count = near_ref.shape[0]

    @pl.when(pl.program_id(0) == 0)
    def _():
        cross = jnp.concatenate(
            [
                jnp.concatenate([sums_ref[h, 256:384], sums_ref[h, 384:]], axis=1)
                for h in range(2)
            ]
        )
        for ref, which in ((near_tri_ref, side), (far_tri_ref, 1 - side)):
            for i in range(2):
                for j in range(2):
                    tri[i, :, which, pl.ds(8 * j, 8), :] = ref[
                        :, pl.ds(8 * i, 8), pl.ds(256 * j, 256)
                    ]
        tri_one, tri_two = (split(tri[i].reshape(256, 256)) for i in range(2))
        coeff_two = triple(tri_two, split(sums_ref[1, :256]))
        moved = sums_ref[0, :256] - triple(split(cross), split(coeff_two))
        coeffs[:256] = triple(tri_one, split(moved))
        coeffs[256:] = coeff_two

    right = split(coeffs[...])
    for ref, which in ((near_ref, side), (far_ref, 1 - side)):
        panel = ref[:, :ROWS, :].reshape(count * ROWS, 512)
        change = triple(split(panel), right).reshape(count, ROWS, 128)
        out_ref[:, which] = old_ref[:, which] - change


def update(place, near, far, sums, by_owner):
    count = 4
    return pl.pallas_call(
        update_kernel,
        grid=(NY // count,),
        out_shape=jax.ShapeDtypeStruct(by_owner.shape, jnp.float32),
        in_specs=[
            pl.BlockSpec(memory_space=pltpu.SMEM),
            pl.BlockSpec((count, ROWS + 16, 512), lambda i: (i, 0, 0)),
            pl.BlockSpec((count, ROWS + 16, 512), lambda i: (i, 0, 0)),
            pl.BlockSpec((2, 512, 128), lambda i: (0, 0, 0)),
            pl.BlockSpec((NY, 16, 512), lambda i: (0, ROWS // 16, 0)),
            pl.BlockSpec((NY, 16, 512), lambda i: (0, ROWS // 16, 0)),
            pl.BlockSpec((count, 2, ROWS, 128), lambda i: (i, 0, 0, 0)),
        ],
        out_specs=pl.BlockSpec((count, 2, ROWS, 128), lambda i: (i, 0, 0, 0)),
        scratch_shapes=[
            pltpu.VMEM((512, 128), jnp.float32),
            pltpu.VMEM((2, NY, 2, 16, 256), jnp.float32),
        ],
        compiler_params=pltpu.CompilerParams(vmem_limit_bytes=60 * MIB),
        name="update",
    )(place, near, far, sums, near, far, by_owner)


def shards(vectors, panel_one, factor_one, panel_two, factor_two):
    side, core = lax.axis_index("xh"), lax.axis_index("core")
    place = jnp.stack([side, core]).astype(jnp.int32)

    own = pack(panel_one, panel_two, factor_one, factor_two)
    near = lax.all_gather(own, "y", axis=0)
    by_owner = vectors.reshape(NY, 2, ROWS, 128)
    theirs = lax.dynamic_index_in_dim(by_owner, 1 - side, 1, False)
    seen = swap(theirs, "xh")
    far = lax.all_gather(swap(own, "xh"), "y", axis=0)

    keep, send = products(place, near, by_owner, seen)
    part = keep + swap(send, "core")
    inner = part[:512].reshape(2, 16, 16, 128).transpose(1, 0, 2, 3)
    cross = jnp.broadcast_to(part[512:].reshape(16, 1, 16, 128), (16, 2, 16, 128))
    parts = jnp.concatenate([inner, cross], axis=2).reshape(32, 32, 128)
    parts = lax.all_to_all(parts, ("xl", "z", "xh"), 0, 0)
    spread = jnp.broadcast_to(parts.sum(0)[None], (16, 32, 128))
    part = lax.all_to_all(spread, ("xl", "z"), 0, 0)
    part = part.reshape(16, 2, 16, 128).transpose(1, 0, 2, 3).reshape(512, 128)
    sums = lax.all_gather(part, "core", axis=0)
    return update(place, near, far, sums, by_owner).reshape(vectors.shape)


def solution(mesh):
    fine = Mesh(mesh.devices.reshape(SIZES), AXES)
    prow, pcol = ("xl", "z", "core"), ("y", "xh")
    in_specs = (
        P(prow, pcol),
        P(prow + pcol, None),
        P(pcol, None),
        P(prow + pcol, None),
        P(pcol, None),
    )
    return jax.shard_map(
        shards,
        mesh=fine,
        in_specs=in_specs,
        out_specs=P(prow, pcol),
        check_vma=False,
    )
```

```python
import functools

import jax
import jax.numpy as jnp
from jax import lax
from jax.experimental import pallas as pl
from jax.experimental.pallas import tpu as pltpu
from jax.sharding import Mesh
from jax.sharding import PartitionSpec as P

AXES = ("xl", "z", "core", "y", "xh")
SIZES = (2, 8, 2, 8, 2)
NY = 8
ROWS = 192
MIB = 1024 * 1024


def swap(value, axis):
    return lax.ppermute(value, axis, [(0, 1), (1, 0)])


def together(*values):
    return lax.optimization_barrier(values)


def split(value):
    high = value.astype(jnp.bfloat16)
    return high, (value - high.astype(jnp.float32)).astype(jnp.bfloat16)


def pack_kernel(one_ref, two_ref, out_ref):
    out_ref[:, :256] = one_ref[...]
    out_ref[:, 256:] = two_ref[...]


def pack(panel_one, panel_two):
    vmem = pl.BlockSpec(memory_space=pltpu.VMEM)
    return pl.pallas_call(
        pack_kernel,
        out_shape=jax.ShapeDtypeStruct((ROWS, 512), jnp.float32),
        in_specs=[vmem] * 2,
        out_specs=vmem,
        name="pack",
    )(panel_one, panel_two)


def products_kernel(
    place_ref, near_ref, mine_ref, seen_ref, keep_ref, send_ref, inner, cross
):
    side, core = place_ref[0], place_ref[1]
    step = pl.program_id(0)
    count = near_ref.shape[0]
    left = near_ref[...].reshape(count * ROWS, 512)
    right = jnp.concatenate(
        [
            mine_ref[:, side].reshape(count * ROWS, 128),
            seen_ref[...].reshape(count * ROWS, 128),
        ],
        axis=1,
    )
    high, low = split(left)
    right_high, right_low = split(right)
    by_rows = (((0,), (0,)), ((), ()))

    def triple(a, a_low, b, b_low):
        return lax.dot_general(
            jnp.concatenate([a, a, a_low]),
            jnp.concatenate([b, b_low, b]),
            by_rows,
            preferred_element_type=jnp.float32,
        )

    inner_part = triple(high, low, right_high, right_low)
    cross_part = triple(high[:, :256], low[:, :256], high[:, 256:], low[:, 256:])
    inner_part = inner_part.reshape(2, 256, 256)
    cross_part = cross_part.reshape(2, 128, 256)

    @pl.when(step == 0)
    def _():
        inner[...] = inner_part
        cross[...] = cross_part

    @pl.when(step > 0)
    def _():
        inner[...] += inner_part
        cross[...] += cross_part

    @pl.when(step == pl.num_programs(0) - 1)
    def _():
        for out_ref, which in ((keep_ref, core), (send_ref, 1 - core)):
            own, far = inner[which, :, :128], inner[which, :, 128:]
            out_ref[:256] = jnp.where(side == 0, own, far)
            out_ref[256:512] = jnp.where(side == 0, far, own)
            out_ref[512:640] = cross[which, :, :128]
            out_ref[640:] = cross[which, :, 128:]


def products(place, near, by_owner, seen):
    count = 4
    return pl.pallas_call(
        products_kernel,
        grid=(NY // count,),
        out_shape=[jax.ShapeDtypeStruct((768, 128), jnp.float32)] * 2,
        in_specs=[
            pl.BlockSpec(memory_space=pltpu.SMEM),
            pl.BlockSpec((count, ROWS, 512), lambda i: (i, 0, 0)),
            pl.BlockSpec((count, 2, ROWS, 128), lambda i: (i, 0, 0, 0)),
            pl.BlockSpec((count, ROWS, 128), lambda i: (i, 0, 0)),
        ],
        out_specs=[pl.BlockSpec((768, 128), lambda i: (0, 0))] * 2,
        scratch_shapes=[
            pltpu.VMEM((2, 256, 256), jnp.float32),
            pltpu.VMEM((2, 128, 256), jnp.float32),
        ],
        compiler_params=pltpu.CompilerParams(vmem_limit_bytes=48 * MIB),
        name="products",
    )(place, near, by_owner, seen)


def triple(left, right):
    (high, low), (right_high, right_low) = left, right
    both = jnp.concatenate([right_high, right_low], axis=1)
    main = jnp.dot(high, both, preferred_element_type=jnp.float32)
    rest = jnp.dot(low, right_high, preferred_element_type=jnp.float32)
    return main[:, :128] + (main[:, 128:] + rest)


def update_kernel(
    place_ref, near_ref, far_ref, sums_ref, tri_ref, old_ref, out_ref, coeffs
):
    side = place_ref[0]
    count = near_ref.shape[0]

    @pl.when(pl.program_id(0) == 0)
    def _():
        cross = jnp.concatenate(
            [
                jnp.concatenate([sums_ref[h, 256:384], sums_ref[h, 384:]], axis=1)
                for h in range(2)
            ]
        )
        coeff_two = triple(split(tri_ref[1]), split(sums_ref[1, :256]))
        moved = sums_ref[0, :256] - triple(split(cross), split(coeff_two))
        coeffs[:256] = triple(split(tri_ref[0]), split(moved))
        coeffs[256:] = coeff_two

    right = split(coeffs[...])
    for ref, which in ((near_ref, side), (far_ref, 1 - side)):
        panel = ref[...].reshape(count * ROWS, 512)
        change = triple(split(panel), right).reshape(count, ROWS, 128)
        out_ref[:, which] = old_ref[:, which] - change


def update(place, near, far, sums, tri, by_owner):
    count = 4
    return pl.pallas_call(
        update_kernel,
        grid=(NY // count,),
        out_shape=jax.ShapeDtypeStruct(by_owner.shape, jnp.float32),
        in_specs=[
            pl.BlockSpec(memory_space=pltpu.SMEM),
            pl.BlockSpec((count, ROWS, 512), lambda i: (i, 0, 0)),
            pl.BlockSpec((count, ROWS, 512), lambda i: (i, 0, 0)),
            pl.BlockSpec((2, 512, 128), lambda i: (0, 0, 0)),
            pl.BlockSpec((2, 256, 256), lambda i: (0, 0, 0)),
            pl.BlockSpec((count, 2, ROWS, 128), lambda i: (i, 0, 0, 0)),
        ],
        out_specs=pl.BlockSpec((count, 2, ROWS, 128), lambda i: (i, 0, 0, 0)),
        scratch_shapes=[pltpu.VMEM((512, 128), jnp.float32)],
        compiler_params=pltpu.CompilerParams(vmem_limit_bytes=60 * MIB),
        name="update",
    )(place, near, far, sums, tri, by_owner)


def shards(vectors, panel_one, factor_one, panel_two, factor_two):
    side, core = lax.axis_index("xh"), lax.axis_index("core")
    place = jnp.stack([side, core]).astype(jnp.int32)

    own = pack(panel_one, panel_two)
    near = lax.all_gather(own, "y", axis=0)
    by_owner = vectors.reshape(NY, 2, ROWS, 128)
    theirs = lax.dynamic_index_in_dim(by_owner, 1 - side, 1, False)
    seen = swap(theirs, "xh")

    tri = jnp.where(core == 0, factor_one, factor_two).reshape(8, 4, 128)
    tri = lax.dynamic_index_in_dim(tri, lax.axis_index("z"), 0, False)
    tri, _ = together(jnp.broadcast_to(tri[None], (16, 4, 128)), own)
    tri = lax.all_to_all(tri, ("y", "xh"), 0, 0).reshape(64, 128)
    far, tri = together(swap(own, "xh"), tri)
    far = lax.all_gather(far, "y", axis=0)
    tri = jnp.broadcast_to(tri[None], (8, 64, 128))
    tri = lax.all_to_all(tri, "z", 0, 0).reshape(8, 16, 2, 256)
    tri = tri.transpose(1, 0, 2, 3).reshape(256, 256)
    tri = lax.all_gather(tri, "core", axis=0)
    near, tri = together(near, tri)

    keep, send = products(place, near, by_owner, seen)
    part = keep + swap(send, "core")
    inner = part[:512].reshape(2, 16, 16, 128).transpose(1, 0, 2, 3)
    cross = jnp.broadcast_to(part[512:].reshape(16, 1, 16, 128), (16, 2, 16, 128))
    parts = jnp.concatenate([inner, cross], axis=2).reshape(32, 32, 128)
    parts = lax.all_to_all(parts, ("xl", "z", "xh"), 0, 0)
    spread = jnp.broadcast_to(parts.sum(0)[None], (16, 32, 128))
    part = lax.all_to_all(spread, ("xl", "z"), 0, 0)
    part = part.reshape(16, 2, 16, 128).transpose(1, 0, 2, 3).reshape(512, 128)
    sums = lax.all_gather(part, "core", axis=0)
    return update(place, near, far, sums, tri, by_owner).reshape(vectors.shape)


def solution(mesh):
    fine = Mesh(mesh.devices.reshape(SIZES), AXES)
    prow, pcol = ("xl", "z", "core"), ("y", "xh")
    in_specs = (
        P(prow, pcol),
        P(prow + pcol, None),
        P(pcol, None),
        P(prow + pcol, None),
        P(pcol, None),
    )
    return jax.shard_map(
        shards,
        mesh=fine,
        in_specs=in_specs,
        out_specs=P(prow, pcol),
        check_vma=False,
    )
```

```python
import functools

import jax
import jax.numpy as jnp
from jax import lax
from jax.experimental import pallas as pl
from jax.experimental.pallas import tpu as pltpu
from jax.sharding import Mesh
from jax.sharding import PartitionSpec as P

AXES = ("xl", "z", "core", "y", "xh")
SIZES = (2, 8, 2, 8, 2)
NY = 8
ROWS = 192
MIB = 1024 * 1024


def swap(value, axis):
    return lax.ppermute(value, axis, [(0, 1), (1, 0)])


def together(*values):
    return lax.optimization_barrier(values)


def split(value):
    high = value.astype(jnp.bfloat16)
    return high, (value - high.astype(jnp.float32)).astype(jnp.bfloat16)


def pack_kernel(one_ref, two_ref, out_ref):
    out_ref[:, :256] = one_ref[...]
    out_ref[:, 256:] = two_ref[...]


def pack(panel_one, panel_two):
    vmem = pl.BlockSpec(memory_space=pltpu.VMEM)
    return pl.pallas_call(
        pack_kernel,
        out_shape=jax.ShapeDtypeStruct((ROWS, 512), jnp.float32),
        in_specs=[vmem] * 2,
        out_specs=vmem,
        name="pack",
    )(panel_one, panel_two)


def products_kernel(
    place_ref, near_ref, mine_ref, seen_ref, keep_ref, send_ref, inner, cross
):
    side, core = place_ref[0], place_ref[1]
    step = pl.program_id(0)
    count = near_ref.shape[0]
    left = near_ref[...].reshape(count * ROWS, 512)
    right = jnp.concatenate(
        [
            mine_ref[:, side].reshape(count * ROWS, 128),
            seen_ref[...].reshape(count * ROWS, 128),
        ],
        axis=1,
    )
    high, low = split(left)
    right_high, right_low = split(right)
    by_rows = (((0,), (0,)), ((), ()))

    def triple(a, a_low, b, b_low):
        return lax.dot_general(
            jnp.concatenate([a, a, a_low]),
            jnp.concatenate([b, b_low, b]),
            by_rows,
            preferred_element_type=jnp.float32,
        )

    inner_part = triple(high, low, right_high, right_low)
    cross_part = triple(high[:, :256], low[:, :256], high[:, 256:], low[:, 256:])
    inner_part = inner_part.reshape(2, 256, 256)
    cross_part = cross_part.reshape(2, 128, 256)

    @pl.when(step == 0)
    def _():
        inner[...] = inner_part
        cross[...] = cross_part

    @pl.when(step > 0)
    def _():
        inner[...] += inner_part
        cross[...] += cross_part

    @pl.when(step == pl.num_programs(0) - 1)
    def _():
        for out_ref, which in ((keep_ref, core), (send_ref, 1 - core)):
            own, far = inner[which, :, :128], inner[which, :, 128:]
            out_ref[:256] = jnp.where(side == 0, own, far)
            out_ref[256:512] = jnp.where(side == 0, far, own)
            out_ref[512:640] = cross[which, :, :128]
            out_ref[640:] = cross[which, :, 128:]


def products(place, near, by_owner, seen):
    count = 4
    return pl.pallas_call(
        products_kernel,
        grid=(NY // count,),
        out_shape=[jax.ShapeDtypeStruct((768, 128), jnp.float32)] * 2,
        in_specs=[
            pl.BlockSpec(memory_space=pltpu.SMEM),
            pl.BlockSpec((count, ROWS, 512), lambda i: (i, 0, 0)),
            pl.BlockSpec((count, 2, ROWS, 128), lambda i: (i, 0, 0, 0)),
            pl.BlockSpec((count, ROWS, 128), lambda i: (i, 0, 0)),
        ],
        out_specs=[pl.BlockSpec((768, 128), lambda i: (0, 0))] * 2,
        scratch_shapes=[
            pltpu.VMEM((2, 256, 256), jnp.float32),
            pltpu.VMEM((2, 128, 256), jnp.float32),
        ],
        compiler_params=pltpu.CompilerParams(vmem_limit_bytes=48 * MIB),
        name="products",
    )(place, near, by_owner, seen)


def triple(left, right):
    (high, low), (right_high, right_low) = left, right
    both = jnp.concatenate([right_high, right_low], axis=1)
    main = jnp.dot(high, both, preferred_element_type=jnp.float32)
    rest = jnp.dot(low, right_high, preferred_element_type=jnp.float32)
    return main[:, :128] + (main[:, 128:] + rest)


def update_kernel(
    place_ref, near_ref, far_ref, sums_ref, tri_ref, old_ref, out_ref, coeffs
):
    side = place_ref[0]
    count = near_ref.shape[0]

    @pl.when(pl.program_id(0) == 0)
    def _():
        cross = jnp.concatenate(
            [
                jnp.concatenate([sums_ref[h, 256:384], sums_ref[h, 384:]], axis=1)
                for h in range(2)
            ]
        )
        coeff_two = triple(split(tri_ref[1]), split(sums_ref[1, :256]))
        moved = sums_ref[0, :256] - triple(split(cross), split(coeff_two))
        coeffs[:256] = triple(split(tri_ref[0]), split(moved))
        coeffs[256:] = coeff_two

    right = split(coeffs[...])
    for ref, which in ((near_ref, side), (far_ref, 1 - side)):
        panel = ref[...].reshape(count * ROWS, 512)
        change = triple(split(panel), right).reshape(count, ROWS, 128)
        out_ref[:, which] = old_ref[:, which] - change


def update(place, near, far, sums, tri, by_owner):
    count = 4
    return pl.pallas_call(
        update_kernel,
        grid=(NY // count,),
        out_shape=jax.ShapeDtypeStruct(by_owner.shape, jnp.float32),
        in_specs=[
            pl.BlockSpec(memory_space=pltpu.SMEM),
            pl.BlockSpec((count, ROWS, 512), lambda i: (i, 0, 0)),
            pl.BlockSpec((count, ROWS, 512), lambda i: (i, 0, 0)),
            pl.BlockSpec((2, 512, 128), lambda i: (0, 0, 0)),
            pl.BlockSpec((2, 256, 256), lambda i: (0, 0, 0)),
            pl.BlockSpec((count, 2, ROWS, 128), lambda i: (i, 0, 0, 0)),
        ],
        out_specs=pl.BlockSpec((count, 2, ROWS, 128), lambda i: (i, 0, 0, 0)),
        scratch_shapes=[pltpu.VMEM((512, 128), jnp.float32)],
        compiler_params=pltpu.CompilerParams(vmem_limit_bytes=60 * MIB),
        name="update",
    )(place, near, far, sums, tri, by_owner)


def shards(vectors, panel_one, factor_one, panel_two, factor_two):
    side, core = lax.axis_index("xh"), lax.axis_index("core")
    place = jnp.stack([side, core]).astype(jnp.int32)

    own = pack(panel_one, panel_two)
    near = lax.all_gather(own, "y", axis=0)
    by_owner = vectors.reshape(NY, 2, ROWS, 128)
    theirs = lax.dynamic_index_in_dim(by_owner, 1 - side, 1, False)
    seen = swap(theirs, "xh")

    tri = jnp.where(core == 0, factor_one, factor_two).reshape(8, 4, 128)
    tri = lax.dynamic_index_in_dim(tri, lax.axis_index("z"), 0, False)
    tri, _ = together(jnp.broadcast_to(tri[None], (16, 4, 128)), own)
    tri = lax.all_to_all(tri, ("y", "xh"), 0, 0).reshape(64, 128)
    far, tri = together(swap(own, "xh"), tri)
    far = lax.all_gather(far, "y", axis=0)
    tri = jnp.broadcast_to(tri[None], (8, 64, 128))
    tri = lax.all_to_all(tri, "z", 0, 0).reshape(8, 16, 2, 256)
    tri = tri.transpose(1, 0, 2, 3).reshape(256, 256)
    tri = lax.all_gather(tri, "core", axis=0)
    near, tri = together(near, tri)

    keep, send = products(place, near, by_owner, seen)
    sent = lax.all_gather(send, "core", axis=0)
    part = keep + lax.dynamic_index_in_dim(sent, 1 - core, 0, False)
    inner = part[:512].reshape(2, 16, 16, 128).transpose(1, 0, 2, 3)
    cross = jnp.broadcast_to(part[512:].reshape(16, 1, 16, 128), (16, 2, 16, 128))
    parts = jnp.concatenate([inner, cross], axis=2).reshape(32, 32, 128)
    parts = lax.all_to_all(parts, ("xl", "z", "xh"), 0, 0)
    spread = jnp.broadcast_to(parts.sum(0)[None], (16, 32, 128))
    part = lax.all_to_all(spread, ("xl", "z"), 0, 0)
    part = part.reshape(16, 2, 16, 128).transpose(1, 0, 2, 3).reshape(512, 128)
    sums = lax.all_gather(part, "core", axis=0)
    return update(place, near, far, sums, tri, by_owner).reshape(vectors.shape)


def solution(mesh):
    fine = Mesh(mesh.devices.reshape(SIZES), AXES)
    prow, pcol = ("xl", "z", "core"), ("y", "xh")
    in_specs = (
        P(prow, pcol),
        P(prow + pcol, None),
        P(pcol, None),
        P(prow + pcol, None),
        P(pcol, None),
    )
    return jax.shard_map(
        shards,
        mesh=fine,
        in_specs=in_specs,
        out_specs=P(prow, pcol),
        check_vma=False,
    )
```

```python
import functools

import jax
import jax.numpy as jnp
from jax import lax
from jax.experimental import pallas as pl
from jax.experimental.pallas import tpu as pltpu
from jax.sharding import Mesh
from jax.sharding import PartitionSpec as P

AXES = ("xl", "z", "core", "y", "xh")
SIZES = (2, 8, 2, 8, 2)
NY = 8
ROWS = 192
MIB = 1024 * 1024


def swap(value, axis):
    return lax.ppermute(value, axis, [(0, 1), (1, 0)])


def together(*values):
    return lax.optimization_barrier(values)


def split(value):
    high = value.astype(jnp.bfloat16)
    return high, (value - high.astype(jnp.float32)).astype(jnp.bfloat16)


def pack_kernel(one_ref, two_ref, out_ref):
    out_ref[:, :256] = one_ref[...]
    out_ref[:, 256:] = two_ref[...]


def pack(panel_one, panel_two):
    vmem = pl.BlockSpec(memory_space=pltpu.VMEM)
    return pl.pallas_call(
        pack_kernel,
        out_shape=jax.ShapeDtypeStruct((ROWS, 512), jnp.float32),
        in_specs=[vmem] * 2,
        out_specs=vmem,
        name="pack",
    )(panel_one, panel_two)


def streams(count, parts, shape):
    def part(j):
        rest = (0,) * len(shape)
        return pl.BlockSpec((count // parts, *shape), lambda i: (parts * i + j, *rest))

    return [part(j) for j in range(parts)]


def products_kernel(place_ref, *refs):
    *near_refs, mine_ref, seen_ref, keep_ref, send_ref, inner, cross = refs
    side, core = place_ref[0], place_ref[1]
    step = pl.program_id(0)
    count = mine_ref.shape[0]
    left = jnp.concatenate([ref[...].reshape(-1, 512) for ref in near_refs])
    right = jnp.concatenate(
        [
            mine_ref[:, side].reshape(count * ROWS, 128),
            seen_ref[...].reshape(count * ROWS, 128),
        ],
        axis=1,
    )
    high, low = split(left)
    right_high, right_low = split(right)
    by_rows = (((0,), (0,)), ((), ()))

    def triple(a, a_low, b, b_low):
        return lax.dot_general(
            jnp.concatenate([a, a, a_low]),
            jnp.concatenate([b, b_low, b]),
            by_rows,
            preferred_element_type=jnp.float32,
        )

    inner_part = triple(high, low, right_high, right_low)
    cross_part = triple(high[:, :256], low[:, :256], high[:, 256:], low[:, 256:])
    inner_part = inner_part.reshape(2, 256, 256)
    cross_part = cross_part.reshape(2, 128, 256)

    @pl.when(step == 0)
    def _():
        inner[...] = inner_part
        cross[...] = cross_part

    @pl.when(step > 0)
    def _():
        inner[...] += inner_part
        cross[...] += cross_part

    @pl.when(step == pl.num_programs(0) - 1)
    def _():
        for out_ref, which in ((keep_ref, core), (send_ref, 1 - core)):
            own, far = inner[which, :, :128], inner[which, :, 128:]
            out_ref[:256] = jnp.where(side == 0, own, far)
            out_ref[256:512] = jnp.where(side == 0, far, own)
            out_ref[512:640] = cross[which, :, :128]
            out_ref[640:] = cross[which, :, 128:]


def products(place, near, by_owner, seen):
    count = 4
    return pl.pallas_call(
        products_kernel,
        grid=(NY // count,),
        out_shape=[jax.ShapeDtypeStruct((768, 128), jnp.float32)] * 2,
        in_specs=[
            pl.BlockSpec(memory_space=pltpu.SMEM),
            *streams(count, 1, (ROWS, 512)),
            pl.BlockSpec((count, 2, ROWS, 128), lambda i: (i, 0, 0, 0)),
            pl.BlockSpec((count, ROWS, 128), lambda i: (i, 0, 0)),
        ],
        out_specs=[pl.BlockSpec((768, 128), lambda i: (0, 0))] * 2,
        scratch_shapes=[
            pltpu.VMEM((2, 256, 256), jnp.float32),
            pltpu.VMEM((2, 128, 256), jnp.float32),
        ],
        compiler_params=pltpu.CompilerParams(vmem_limit_bytes=48 * MIB),
        name="products",
    )(place, near, by_owner, seen)


def triple(left, right):
    (high, low), (right_high, right_low) = left, right
    both = jnp.concatenate([right_high, right_low], axis=1)
    main = jnp.dot(high, both, preferred_element_type=jnp.float32)
    rest = jnp.dot(low, right_high, preferred_element_type=jnp.float32)
    return main[:, :128] + (main[:, 128:] + rest)


def update_kernel(
    place_ref, sums_ref, tri_ref, *refs
):
    *refs, out_ref, coeffs = refs
    parts = len(refs) // 3
    near_refs, far_refs, old_refs = refs[:parts], refs[parts : 2 * parts], refs[2 * parts :]
    side = place_ref[0]
    count = near_refs[0].shape[0]

    @pl.when(pl.program_id(0) == 0)
    def _():
        cross = jnp.concatenate(
            [
                jnp.concatenate([sums_ref[h, 256:384], sums_ref[h, 384:]], axis=1)
                for h in range(2)
            ]
        )
        coeff_two = triple(split(tri_ref[1]), split(sums_ref[1, :256]))
        moved = sums_ref[0, :256] - triple(split(cross), split(coeff_two))
        coeffs[:256] = triple(split(tri_ref[0]), split(moved))
        coeffs[256:] = coeff_two

    right = split(coeffs[...])
    for j, old_ref in enumerate(old_refs):
        for ref, which in ((near_refs[j], side), (far_refs[j], 1 - side)):
            panel = ref[...].reshape(count * ROWS, 512)
            change = triple(split(panel), right).reshape(count, ROWS, 128)
            out_ref[pl.ds(j * count, count), which] = old_ref[:, which] - change


def update(place, near, far, sums, tri, by_owner):
    count = 4
    return pl.pallas_call(
        update_kernel,
        grid=(NY // count,),
        out_shape=jax.ShapeDtypeStruct(by_owner.shape, jnp.float32),
        in_specs=[
            pl.BlockSpec(memory_space=pltpu.SMEM),
            pl.BlockSpec((2, 512, 128), lambda i: (0, 0, 0)),
            pl.BlockSpec((2, 256, 256), lambda i: (0, 0, 0)),
            *streams(count, 4, (ROWS, 512)),
            *streams(count, 4, (ROWS, 512)),
            *streams(count, 4, (2, ROWS, 128)),
        ],
        out_specs=pl.BlockSpec((count, 2, ROWS, 128), lambda i: (i, 0, 0, 0)),
        scratch_shapes=[pltpu.VMEM((512, 128), jnp.float32)],
        compiler_params=pltpu.CompilerParams(vmem_limit_bytes=60 * MIB),
        name="update",
    )(place, sums, tri, *[near] * 4, *[far] * 4, *[by_owner] * 4)


def shards(vectors, panel_one, factor_one, panel_two, factor_two):
    side, core = lax.axis_index("xh"), lax.axis_index("core")
    place = jnp.stack([side, core]).astype(jnp.int32)

    own = pack(panel_one, panel_two)
    near = lax.all_gather(own, "y", axis=0)
    by_owner = vectors.reshape(NY, 2, ROWS, 128)
    theirs = lax.dynamic_index_in_dim(by_owner, 1 - side, 1, False)
    seen = swap(theirs, "xh")

    tri = jnp.where(core == 0, factor_one, factor_two).reshape(8, 4, 128)
    tri = lax.dynamic_index_in_dim(tri, lax.axis_index("z"), 0, False)
    tri, _ = together(jnp.broadcast_to(tri[None], (16, 4, 128)), own)
    tri = lax.all_to_all(tri, ("y", "xh"), 0, 0).reshape(64, 128)
    far, tri = together(swap(own, "xh"), tri)
    far = lax.all_gather(far, "y", axis=0)
    tri = jnp.broadcast_to(tri[None], (8, 64, 128))
    tri = lax.all_to_all(tri, "z", 0, 0).reshape(8, 16, 2, 256)
    tri = tri.transpose(1, 0, 2, 3).reshape(256, 256)
    tri = lax.all_gather(tri, "core", axis=0)
    near, tri = together(near, tri)

    keep, send = products(place, near, by_owner, seen)
    sent = lax.all_gather(send, "core", axis=0)
    part = keep + lax.dynamic_index_in_dim(sent, 1 - core, 0, False)
    inner = part[:512].reshape(2, 16, 16, 128).transpose(1, 0, 2, 3)
    cross = jnp.broadcast_to(part[512:].reshape(16, 1, 16, 128), (16, 2, 16, 128))
    parts = jnp.concatenate([inner, cross], axis=2).reshape(32, 32, 128)
    parts = lax.all_to_all(parts, ("xl", "z", "xh"), 0, 0)
    spread = jnp.broadcast_to(parts.sum(0)[None], (16, 32, 128))
    part = lax.all_to_all(spread, ("xl", "z"), 0, 0)
    part = part.reshape(16, 2, 16, 128).transpose(1, 0, 2, 3).reshape(512, 128)
    sums = lax.all_gather(part, "core", axis=0)
    return update(place, near, far, sums, tri, by_owner).reshape(vectors.shape)


def solution(mesh):
    fine = Mesh(mesh.devices.reshape(SIZES), AXES)
    prow, pcol = ("xl", "z", "core"), ("y", "xh")
    in_specs = (
        P(prow, pcol),
        P(prow + pcol, None),
        P(pcol, None),
        P(prow + pcol, None),
        P(pcol, None),
    )
    return jax.shard_map(
        shards,
        mesh=fine,
        in_specs=in_specs,
        out_specs=P(prow, pcol),
        check_vma=False,
    )
```

```python
import functools

import jax
import jax.numpy as jnp
from jax import lax
from jax.experimental import pallas as pl
from jax.experimental.pallas import tpu as pltpu
from jax.sharding import Mesh
from jax.sharding import PartitionSpec as P

AXES = ("xl", "z", "core", "y", "xh")
SIZES = (2, 8, 2, 8, 2)
NY = 8
ROWS = 192
MIB = 1024 * 1024


def swap(value, axis):
    return lax.ppermute(value, axis, [(0, 1), (1, 0)])


def together(*values):
    return lax.optimization_barrier(values)


def split(value):
    high = value.astype(jnp.bfloat16)
    return high, (value - high.astype(jnp.float32)).astype(jnp.bfloat16)


def pack_kernel(one_ref, two_ref, out_ref):
    out_ref[:, :256] = one_ref[...]
    out_ref[:, 256:] = two_ref[...]


def pack(panel_one, panel_two):
    vmem = pl.BlockSpec(memory_space=pltpu.VMEM)
    return pl.pallas_call(
        pack_kernel,
        out_shape=jax.ShapeDtypeStruct((ROWS, 512), jnp.float32),
        in_specs=[vmem] * 2,
        out_specs=vmem,
        name="pack",
    )(panel_one, panel_two)


def streams(count, parts, shape):
    def part(j):
        rest = (0,) * len(shape)
        return pl.BlockSpec((count // parts, *shape), lambda i: (parts * i + j, *rest))

    return [part(j) for j in range(parts)]


def products_kernel(place_ref, *refs):
    *near_refs, mine_ref, seen_ref, keep_ref, send_ref, inner, cross = refs
    side, core = place_ref[0], place_ref[1]
    step = pl.program_id(0)
    count = mine_ref.shape[0]
    left = jnp.concatenate([ref[...].reshape(-1, 512) for ref in near_refs])
    right = jnp.concatenate(
        [
            mine_ref[:, side].reshape(count * ROWS, 128),
            seen_ref[...].reshape(count * ROWS, 128),
        ],
        axis=1,
    )
    high, low = split(left)
    right_high, right_low = split(right)
    by_rows = (((0,), (0,)), ((), ()))

    def triple(a, a_low, b, b_low):
        return lax.dot_general(
            jnp.concatenate([a, a, a_low]),
            jnp.concatenate([b, b_low, b]),
            by_rows,
            preferred_element_type=jnp.float32,
        )

    inner_part = triple(high, low, right_high, right_low)
    cross_part = triple(high[:, :256], low[:, :256], high[:, 256:], low[:, 256:])
    inner_part = inner_part.reshape(2, 256, 256)
    cross_part = cross_part.reshape(2, 128, 256)

    @pl.when(step == 0)
    def _():
        inner[...] = inner_part
        cross[...] = cross_part

    @pl.when(step > 0)
    def _():
        inner[...] += inner_part
        cross[...] += cross_part

    @pl.when(step == pl.num_programs(0) - 1)
    def _():
        for out_ref, which in ((keep_ref, core), (send_ref, 1 - core)):
            own, far = inner[which, :, :128], inner[which, :, 128:]
            out_ref[:, 0] = jnp.where(side == 0, own, far).reshape(16, 16, 128)
            out_ref[:, 1] = jnp.where(side == 0, far, own).reshape(16, 16, 128)
            out_ref[:8, 2] = cross[which, :, :128].reshape(8, 16, 128)
            out_ref[8:, 2] = cross[which, :, 128:].reshape(8, 16, 128)


def products(place, near, by_owner, seen):
    count = 4
    return pl.pallas_call(
        products_kernel,
        grid=(NY // count,),
        out_shape=[jax.ShapeDtypeStruct((16, 3, 16, 128), jnp.float32)] * 2,
        in_specs=[
            pl.BlockSpec(memory_space=pltpu.SMEM),
            *streams(count, 1, (ROWS, 512)),
            pl.BlockSpec((count, 2, ROWS, 128), lambda i: (i, 0, 0, 0)),
            pl.BlockSpec((count, ROWS, 128), lambda i: (i, 0, 0)),
        ],
        out_specs=[pl.BlockSpec((16, 3, 16, 128), lambda i: (0, 0, 0, 0))] * 2,
        scratch_shapes=[
            pltpu.VMEM((2, 256, 256), jnp.float32),
            pltpu.VMEM((2, 128, 256), jnp.float32),
        ],
        compiler_params=pltpu.CompilerParams(vmem_limit_bytes=48 * MIB),
        name="products",
    )(place, near, by_owner, seen)


def triple(left, right):
    (high, low), (right_high, right_low) = left, right
    both = jnp.concatenate([right_high, right_low], axis=1)
    main = jnp.dot(high, both, preferred_element_type=jnp.float32)
    rest = jnp.dot(low, right_high, preferred_element_type=jnp.float32)
    return main[:, :128] + (main[:, 128:] + rest)


def update_kernel(
    place_ref, sums_ref, tri_ref, *refs
):
    *refs, out_ref, coeffs = refs
    parts = len(refs) // 3
    near_refs, far_refs, old_refs = refs[:parts], refs[parts : 2 * parts], refs[2 * parts :]
    side = place_ref[0]
    count = near_refs[0].shape[0]

    @pl.when(pl.program_id(0) == 0)
    def _():
        cross = jnp.concatenate(
            [
                jnp.concatenate([sums_ref[h, 256:384], sums_ref[h, 384:]], axis=1)
                for h in range(2)
            ]
        )
        coeff_two = triple(split(tri_ref[1]), split(sums_ref[1, :256]))
        moved = sums_ref[0, :256] - triple(split(cross), split(coeff_two))
        coeffs[:256] = triple(split(tri_ref[0]), split(moved))
        coeffs[256:] = coeff_two

    right = split(coeffs[...])
    for j, old_ref in enumerate(old_refs):
        for ref, which in ((near_refs[j], side), (far_refs[j], 1 - side)):
            panel = ref[...].reshape(count * ROWS, 512)
            change = triple(split(panel), right).reshape(count, ROWS, 128)
            out_ref[pl.ds(j * count, count), which] = old_ref[:, which] - change


def update(place, near, far, sums, tri, by_owner):
    count = 4
    return pl.pallas_call(
        update_kernel,
        grid=(NY // count,),
        out_shape=jax.ShapeDtypeStruct(by_owner.shape, jnp.float32),
        in_specs=[
            pl.BlockSpec(memory_space=pltpu.SMEM),
            pl.BlockSpec((2, 512, 128), lambda i: (0, 0, 0)),
            pl.BlockSpec((2, 256, 256), lambda i: (0, 0, 0)),
            *streams(count, 4, (ROWS, 512)),
            *streams(count, 4, (ROWS, 512)),
            *streams(count, 4, (2, ROWS, 128)),
        ],
        out_specs=pl.BlockSpec((count, 2, ROWS, 128), lambda i: (i, 0, 0, 0)),
        scratch_shapes=[pltpu.VMEM((512, 128), jnp.float32)],
        compiler_params=pltpu.CompilerParams(vmem_limit_bytes=60 * MIB),
        name="update",
    )(place, sums, tri, *[near] * 4, *[far] * 4, *[by_owner] * 4)


def shards(vectors, panel_one, factor_one, panel_two, factor_two):
    side, core = lax.axis_index("xh"), lax.axis_index("core")
    place = jnp.stack([side, core]).astype(jnp.int32)

    own = pack(panel_one, panel_two)
    near = lax.all_gather(own, "y", axis=0)
    by_owner = vectors.reshape(NY, 2, ROWS, 128)
    theirs = lax.dynamic_index_in_dim(by_owner, 1 - side, 1, False)
    seen = swap(theirs, "xh")

    tri = jnp.where(core == 0, factor_one, factor_two).reshape(8, 4, 128)
    tri = lax.dynamic_index_in_dim(tri, lax.axis_index("z"), 0, False)
    tri, _ = together(jnp.broadcast_to(tri[None], (16, 4, 128)), own)
    tri = lax.all_to_all(tri, ("y", "xh"), 0, 0).reshape(64, 128)
    far, tri = together(swap(own, "xh"), tri)
    far = lax.all_gather(far, "y", axis=0)
    tri = jnp.broadcast_to(tri[None], (8, 64, 128))
    tri = lax.all_to_all(tri, "z", 0, 0).reshape(8, 16, 2, 256)
    tri = tri.transpose(1, 0, 2, 3).reshape(256, 256)
    tri = lax.all_gather(tri, "core", axis=0)
    near, tri = together(near, tri)

    keep, send = products(place, near, by_owner, seen)
    sent = lax.all_gather(send, "core", axis=0)
    part = keep + lax.dynamic_index_in_dim(sent, 1 - core, 0, False)
    cross = jnp.broadcast_to(part[:, 2:], (16, 2, 16, 128))
    parts = jnp.concatenate([part[:, :2], cross], axis=2).reshape(32, 32, 128)
    parts = lax.all_to_all(parts, ("xl", "z", "xh"), 0, 0)
    spread = jnp.broadcast_to(parts.sum(0)[None], (16, 32, 128))
    part = lax.all_to_all(spread, ("xl", "z"), 0, 0)
    part = part.reshape(16, 2, 16, 128).transpose(1, 0, 2, 3).reshape(512, 128)
    sums = lax.all_gather(part, "core", axis=0)
    return update(place, near, far, sums, tri, by_owner).reshape(vectors.shape)


def solution(mesh):
    fine = Mesh(mesh.devices.reshape(SIZES), AXES)
    prow, pcol = ("xl", "z", "core"), ("y", "xh")
    in_specs = (
        P(prow, pcol),
        P(prow + pcol, None),
        P(pcol, None),
        P(prow + pcol, None),
        P(pcol, None),
    )
    return jax.shard_map(
        shards,
        mesh=fine,
        in_specs=in_specs,
        out_specs=P(prow, pcol),
        check_vma=False,
    )
```
